512 devices in a mesh: row: 64 (over z, x, core), grp: 8 (over y).
Axes of the slice: x: 4, y: 8, z: 8, core: 2. Of those that a mesh axis runs over, the one named last changes fastest.
Arguments:
- a_blocks: bfloat16 [4096, 64, 1024], P(('row', 'grp')), may hold values from -0.75 to 0.75
- p_blocks: bfloat16 [4096, 64, 128], P(('row', 'grp')), may hold values from -0.75 to 0.75
- a_cols: int32 [4096, 16], P(('row', 'grp')), may hold values from 0 to 455
- a_live: int32 [512], P(('row', 'grp')), may hold values from 2 to 8, as said below
- group_need: int32 [512, 8, 8], P(('row', 'grp')), may hold values from 0 to 7
- row_send: int32 [512, 64, 6], P(('row', 'grp')), may hold values from 0 to 7
Outputs:
- coarse: bfloat16 [64, 64, 128, 128], P('row', 'grp')
The draws below stay inside these ranges and needn't reach their ends.
Inputs may be any that keep to these rules, and one draw needn't show every extreme that they name: `a_live`: some device has all 8 rows active; the others between a quarter and all of them.
All inputs are finite; a program needn't handle non-finite values.
Results may differ from the reference program's by a relative error of at most 0.015.
Values may be sent and summed in bfloat16 or wider, within the bound.
No kernel may reach another device: no remote copies, remote signals or barrier semaphores. Data moves between devices by JAX's collectives and lax.ppermute only.
A program may use at most 128 MiB of HBM per device.

```python
import jax
import jax.numpy as jnp
from jax import lax

BS = 64
CW = 128
SA = 16
RB = 8
GQ = 8
GP = 6
NB = 4096
TAB = 456
N_ROW = 64
N_GRP = 8


def draw_a_live(key, part):
    key = jax.random.fold_in(key, 11)
    counts = jax.random.randint(key, (N_ROW * N_GRP,), RB // 3, RB + 1)
    fullest = jax.random.randint(jax.random.fold_in(key, 5), (), 0, N_ROW * N_GRP)
    return counts.at[fullest].set(RB).astype(jnp.int32)


def plant(array, key, smallest, largest):
    place = [jax.random.randint(jax.random.fold_in(key, axis), (), 0, length) for axis, length in enumerate(array.shape)]
    widest = array.shape.index(max(array.shape))
    beside = place[:widest] + [(place[widest] + 1) % array.shape[widest]] + place[widest + 1:]
    return array.at[tuple(place)].set(smallest).at[tuple(beside)].set(largest)


def block_scale(own_key, dims, split, least, high):
    def one(axis_at, parts):
        heights = jax.random.uniform(jax.random.fold_in(jax.random.fold_in(own_key, 6), axis_at), (parts,), jnp.float32, least / len(split), high / len(split))
        return jnp.repeat(jnp.exp(heights), dims[axis_at] // parts).reshape((-1,) + (1,) * (len(dims) - axis_at - 1))

    factor_of = one(*split[0])
    for cut in split[1:]:
        factor_of = factor_of * one(*cut)
    return factor_of


def normal_values(key, extent, scale, limit, shards=(), held_as=jnp.bfloat16):
    result = scale * jax.random.normal(key, extent, jnp.float32)
    if shards:
        result = result * block_scale(key, extent, shards, -0.22, 0.18)
    return jnp.clip(result, -limit, limit).astype(held_as)


def setup_inputs(seed: int = 0) -> dict:
    arg_keys = jax.random.split(jax.random.key(seed), 7)
    return {
        "a_blocks": normal_values(arg_keys[0], (NB, BS, SA * BS), BS ** -0.5, 0.75, ((0, 512),)),
        "p_blocks": normal_values(arg_keys[1], (NB, BS, CW), BS ** -0.5, 0.75, ((0, 512),)),
        "a_cols": plant(jax.random.randint(arg_keys[2], (NB, SA), 0, TAB), jax.random.fold_in(arg_keys[2], 1), 0, TAB - 1).astype(jnp.int32),
        "a_live": draw_a_live(jax.random.fold_in(arg_keys[6], 71), 0),
        "group_need": plant(jax.random.randint(arg_keys[4], (N_ROW * N_GRP, N_GRP, GQ), 0, RB), jax.random.fold_in(arg_keys[4], 1), 0, RB - 1).astype(jnp.int32),
        "row_send": plant(jax.random.randint(arg_keys[5], (N_ROW * N_GRP, N_ROW, GP), 0, RB), jax.random.fold_in(arg_keys[5], 1), 0, RB - 1).astype(jnp.int32),
    }


def piece_product(a_blocks, p_blocks, a_cols, a_live, group_need, row_send, group_index, member_index):
    piece = (group_index * N_GRP + member_index).astype(jnp.int32)
    first_row = (piece * RB).astype(jnp.int32)
    own_a = lax.dynamic_slice_in_dim(a_blocks, first_row, RB, 0)
    own_p = lax.dynamic_slice_in_dim(p_blocks, first_row, RB, 0)
    own_cols = lax.dynamic_slice_in_dim(a_cols, first_row, RB, 0)
    own_rows = first_row + jnp.arange(RB, dtype=jnp.int32)
    needed = lax.dynamic_index_in_dim(group_need, piece, 0, keepdims=False)
    sources = (group_index * N_GRP + jnp.arange(N_GRP, dtype=jnp.int32))[:, None] * RB
    near_rows = (sources + needed).reshape(-1)
    sent = row_send.reshape(N_ROW, N_GRP, N_ROW, GP)
    sent = lax.dynamic_index_in_dim(sent, member_index, 1, keepdims=False)
    sent = lax.dynamic_index_in_dim(sent, group_index, 1, keepdims=False)
    senders = (jnp.arange(N_ROW, dtype=jnp.int32) * N_GRP + member_index)[:, None] * RB
    far_rows = (senders + sent).reshape(-1)
    table_rows = jnp.concatenate([own_rows, near_rows, far_rows]).astype(jnp.int32)
    near_panels = jnp.zeros((RB + N_GRP * GQ,), jnp.int32) + group_index
    far_panels = jnp.repeat(jnp.arange(N_ROW, dtype=jnp.int32), GP)
    table_panels = jnp.concatenate([near_panels, far_panels]).astype(jnp.int32)
    block_columns = table_rows[own_cols]
    block_panels = table_panels[own_cols]
    left_side = jnp.einsum('rkc,rkn->rcn', own_p.astype(jnp.float32), own_a.astype(jnp.float32)).astype(jnp.bfloat16)
    left_side = left_side.reshape(RB, CW, SA, BS).astype(jnp.float32)
    right_side = p_blocks[block_columns].astype(jnp.float32)
    products = jnp.einsum('rcsk,rskq->rscq', left_side, right_side)
    live_rows = lax.dynamic_index_in_dim(a_live, piece, 0, keepdims=False)
    active = (jnp.arange(RB, dtype=jnp.int32) < live_rows).astype(jnp.float32)
    products = products * active[:, None, None, None]
    partial_sum = jnp.zeros((N_ROW, CW, CW), jnp.float32).at[block_panels.reshape(-1)].add(products.reshape(-1, CW, CW))
    rounded = lax.optimization_barrier(partial_sum.astype(jnp.bfloat16))
    return rounded.astype(jnp.float32)


def group_panel(arrays, group_index):
    def add_member(running, member_index):
        return running + piece_product(*arrays, group_index, member_index), None
    running, unused = lax.scan(add_member, jnp.zeros((N_ROW, CW, CW), jnp.float32), jnp.arange(N_GRP, dtype=jnp.int32))
    return running.astype(jnp.bfloat16)


def reference(a_blocks, p_blocks, a_cols, a_live, group_need, row_send):
    arrays = (a_blocks, p_blocks, a_cols, a_live, group_need, row_send)
    return lax.map(partial_group(arrays), jnp.arange(N_ROW, dtype=jnp.int32))


def partial_group(arrays):
    def one_group(group_index):
        return group_panel(arrays, group_index)
    return one_group
```

```python
import functools

import jax
import jax.numpy as jnp
from jax import lax
from jax.experimental import pallas as pl
from jax.experimental.pallas import tpu as pltpu
from jax.sharding import Mesh, PartitionSpec as P

NZ, NX, NC, NY = 8, 4, 2, 8
RB, BS, CW, SA = 8, 64, 128, 16
GP = 6
NEAR = RB + NY * RB
SLOTS = RB * SA
PAD = 16
ROWS = RB * BS + PAD
UNROLL = 4
OFF = 255


def terms_kernel(place, code, sent, cols, need, a_ref, p_ref, near_ref, o_ref, left, acc, todo):
    turn = pl.program_id(0)
    my_z, my_x, my_c, live = place[0], place[1], place[2], place[3]

    for n in range(RB):
        rows = pl.ds(n * BS, BS)
        product = lax.dot_general(
            a_ref[0, rows, SA * BS :], a_ref[0, rows, : SA * BS], (((0,), (0,)), ((), ())),
            preferred_element_type=jnp.float32,
        ).astype(jnp.bfloat16)
        for pair in range(SA // 2):
            left[n * (SA // 2) + pair] = product[:, pair * CW : (pair + 1) * CW]
    acc[...] = jnp.zeros_like(acc)

    def add_terms(count, row_of):
        def body(step, unused):
            found = []
            for u in range(UNROLL):
                item = todo[step * UNROLL + u]
                slot = item & (SLOTS - 1)
                block = row_of(item)
                odd = (slot & 1) == 1
                zero = jnp.zeros_like(block)
                right = jnp.concatenate([jnp.where(odd, zero, block), jnp.where(odd, block, zero)], 0)
                found.append((item >> 16, jnp.dot(left[slot >> 1], right, preferred_element_type=jnp.float32)))
            for panel, term in found:
                acc[panel] += term
            return 0

        for u in range(UNROLL):
            todo[count + u] = (NC * NZ) << 16
        lax.fori_loop(0, (count + UNROLL - 1) // UNROLL, body, 0)

    def pick_far(slot, count):
        panel = code[turn, 0, slot]
        listed = code[turn, 1, slot]
        mine = (panel < NZ * NX * NC) & (((panel >> 1) & (NX - 1)) == my_x)
        source = jnp.where(mine, (panel & 1) * NZ + (panel >> 3), 0)
        row = sent[source, (turn * NC + my_c) * GP + listed]
        todo[count] = slot | (row << 8) | (source << 12) | (source << 16)
        return count + mine.astype(jnp.int32)

    far = lax.fori_loop(0, SLOTS, pick_far, 0, unroll=8)
    add_terms(far, lambda item: p_ref[(item >> 12) & 15, pl.ds(pl.multiple_of(((item >> 8) & 7) * BS, BS), BS), :])

    @pl.when(turn == my_x)
    def _():
        own = (my_c * NZ + my_z) << 16

        def pick_near(slot, count):
            entry = cols[slot]
            mine = (entry < NEAR) & ((slot >> 4) < live)
            listed = jnp.where(mine, jnp.maximum(entry - RB, 0), 0)
            member = jnp.where(entry < RB, place[4], listed >> 3)
            row = jnp.where(entry < RB, entry, need[listed])
            todo[count] = slot | (row << 8) | (jnp.where(mine, member, 0) << 12) | own
            return count + mine.astype(jnp.int32)

        close = lax.fori_loop(0, SLOTS, pick_near, 0, unroll=8)
        add_terms(close, lambda item: near_ref[(item >> 12) & 15, pl.ds(pl.multiple_of(((item >> 8) & 7) * BS, BS), BS), :])

    for source in range(NC * NZ):
        o_ref[0, source % NZ, source // NZ] = acc[source].astype(jnp.bfloat16)


def shards(a_blocks, p_blocks, a_cols, a_live, group_need, row_send):
    my_z, my_x, my_c, my_y = (lax.axis_index(axis) for axis in ("z", "x", "c", "y"))
    own_p = p_blocks.reshape(RB * BS, CW)

    lists = row_send.reshape(NZ, NX * NC * GP).astype(jnp.bfloat16)
    lists = jnp.pad(lists[:, None, :], ((0, 0), (0, PAD - 1), (0, CW - NX * NC * GP)))
    message = jnp.concatenate([jnp.broadcast_to(own_p[None], (NZ, RB * BS, CW)), lists], 1)
    far_p = lax.all_to_all(message, "z", split_axis=0, concat_axis=0, tiled=True)
    near_p = lax.all_to_all(message, "y", split_axis=0, concat_axis=0, tiled=True)

    live = jnp.arange(RB, dtype=jnp.int32)[:, None] < a_live[0]
    far = live & (a_cols >= NEAR)
    entry = jnp.where(far, a_cols - NEAR, 0)
    panel = jnp.where(far, entry // GP, OFF)
    codes = jnp.stack([panel.reshape(-1), (entry % GP).reshape(-1)]).astype(jnp.bfloat16)
    codes = jnp.pad(codes, ((0, PAD - 2), (0, SA * BS + CW - SLOTS)))
    rows = jnp.concatenate([a_blocks.reshape(RB * BS, SA * BS), own_p], 1)
    group_rows = lax.all_gather(jnp.concatenate([rows, codes], 0), "x", axis=0)
    far_p = lax.all_gather(far_p, "c", axis=0).reshape(NC * NZ, ROWS, CW)

    code = group_rows[:, RB * BS : RB * BS + 2, :SLOTS].astype(jnp.int32)
    sent = far_p[:, RB * BS, : NX * NC * GP].astype(jnp.int32)
    place = jnp.stack([my_z, my_x, my_c, a_live[0], my_y]).astype(jnp.int32)

    partial = pl.pallas_call(
        terms_kernel,
        out_shape=jax.ShapeDtypeStruct((NX, NZ, NC, CW, CW), jnp.bfloat16),
        grid_spec=pltpu.PrefetchScalarGridSpec(
            num_scalar_prefetch=5,
            grid=(NX,),
            in_specs=[
                pl.BlockSpec((1, ROWS, SA * BS + CW), lambda i, *_: (i, 0, 0)),
                pl.BlockSpec((NC * NZ, ROWS, CW), lambda i, *_: (0, 0, 0)),
                pl.BlockSpec((NY, ROWS, CW), lambda i, *_: (0, 0, 0)),
            ],
            out_specs=pl.BlockSpec((1, NZ, NC, CW, CW), lambda i, *_: (i, 0, 0, 0, 0)),
            scratch_shapes=[
                pltpu.VMEM((RB * SA // 2, CW, CW), jnp.bfloat16),
                pltpu.VMEM((NC * NZ + 1, CW, CW), jnp.float32),
                pltpu.SMEM((SLOTS + UNROLL,), jnp.int32),
            ],
        ),
        compiler_params=pltpu.CompilerParams(vmem_limit_bytes=40 * 1024 * 1024),
        cost_estimate=pl.CostEstimate(flops=2 * 10**9, bytes_accessed=12 * 10**6, transcendentals=0),
        name="terms",
    )(place, code, sent, a_cols.reshape(-1), group_need.reshape(-1), group_rows, far_p, near_p)

    parts = lax.all_to_all(
        partial.reshape(NX * NY, NC, CW, CW), ("x", "y"), split_axis=0, concat_axis=0, tiled=True
    ).reshape(NX, NY, NC, CW, CW)
    total = jnp.sum(parts.astype(jnp.float32), axis=1).astype(jnp.bfloat16)
    return total.reshape(1, NX * NC, CW, CW)


def solution(mesh):
    split = Mesh(mesh.devices.reshape(NZ, NX, NC, NY), ("z", "x", "c", "y"))
    every = ("z", "x", "c", "y")
    placed = (
        P(every, None, None),
        P(every, None, None),
        P(every, None),
        P(every),
        P(every, None, None),
        P(every, None, None),
    )
    return jax.shard_map(
        shards, mesh=split, in_specs=placed, out_specs=P(("z", "x", "c"), "y", None, None), check_vma=False
    )
```

```python
import jax
import jax.numpy as jnp
from jax import lax
from jax.experimental import pallas as pl
from jax.experimental.pallas import tpu as pltpu
from jax.sharding import Mesh, PartitionSpec as P

NZ, NX, NC, NY = 8, 4, 2, 8
RB, BS, CW, SA = 8, 64, 128, 16
GP = 6
NEAR = RB + NY * RB
SLOTS = RB * SA
PAD = 16
PROWS = RB * BS
ROWS = PROWS + PAD
AW = SA * BS + CW
UNROLL = 4
OFF = 255
FLAG = 20
BF16, F32, I32 = jnp.bfloat16, jnp.float32, jnp.int32


def pack_kernel(live, a_ref, p_ref, cols, lists, own_ref, message_ref):
    own_ref[:PROWS, : SA * BS] = a_ref[...]
    own_ref[:PROWS, SA * BS :] = p_ref[...]
    message_ref[:PROWS, :] = p_ref[...]
    listed = jnp.concatenate([lists[z] for z in range(NZ)], 1)
    listed = jnp.concatenate([listed, jnp.zeros((NX * NC, CW - NZ * GP), I32)], 1)
    message_ref[PROWS:, :] = jnp.concatenate([listed, jnp.zeros_like(listed)], 0).astype(F32).astype(BF16)
    entry = cols[...] - NEAR
    far = (entry >= 0) & (lax.broadcasted_iota(I32, (RB, SA), 0) < live[0])
    entry = jnp.where(far, entry, 0)
    panel = (entry * 10923) >> 16
    codes = jnp.concatenate([jnp.where(far, panel, OFF), entry - panel * GP], 0)
    own_ref[PROWS:, :] = jnp.zeros((PAD, AW), BF16)
    own_ref[PROWS:, :SA] = codes.astype(F32).astype(BF16)


def terms_kernel(place, need, cols, *refs):
    groups_hbm, refs = refs[:NX], refs[NX:]
    here_hbm, one_hbm, two_hbm, three_hbm, four_hbm, crossed_hbm, near_hbm = refs[:7]
    o_ref, a_ref, p_ref, near_ref, left, acc, items_v, sent_v, items, sent, todo, sems = refs[7:]
    my_z, my_x, my_c, my_y, live, odd_z = (place[i] for i in range(6))
    back = 2 * my_c - 1
    copies = [pltpu.make_async_copy(groups_hbm[turn], a_ref.at[turn], sems.at[turn]) for turn in range(NX)]
    sources = [(here_hbm, 0), (one_hbm, back), (two_hbm, 2 * back), (three_hbm, 3 * back), (four_hbm, 4)]
    sources += [(crossed_hbm.at[s], -(s + 1) * back) for s in range(3)]
    tables = [
        pltpu.make_async_copy(source, p_ref.at[(my_z + step) & (NZ - 1)], sems.at[NX + at])
        for at, (source, step) in enumerate(sources)
    ]
    near_copy = pltpu.make_async_copy(near_hbm, near_ref, sems.at[NX + NZ])
    for copy in copies[:1] + tables + [near_copy] + copies[1:]:
        copy.start()
    slots = lax.broadcasted_iota(I32, (RB, CW), 0) * SA + lax.broadcasted_iota(I32, (RB, CW), 1)
    moves = [
        pltpu.make_async_copy(items_v.at[turn], items.at[turn], sems.at[NX + NZ + 1 + turn]) for turn in range(NX + 1)
    ]
    list_move = pltpu.make_async_copy(sent_v, sent, sems.at[2 * NX + NZ + 2])

    entry = cols[...]
    close = (entry < NEAR) & (lax.broadcasted_iota(I32, (RB, SA), 0) < live) & ((my_z & 1) == odd_z)
    items_v[NX, :, :SA] = jnp.where(close, slots[:, :SA] | (entry << 7) | (1 << FLAG), 0)
    moves[NX].start()
    acc[...] = jnp.zeros_like(acc)

    for turn in range(NX):
        copies[turn].wait()
        code = a_ref[turn, pl.ds(PROWS, PAD), :CW].astype(F32).astype(I32)
        panel, listed = code[:RB], code[RB:]
        mine = (panel < OFF) & (((panel >> 1) & (NX - 1)) == my_x) & (((panel >> 3) & 1) == odd_z)
        source = (panel >> 3) * NC + (panel & 1)
        item = (slots + turn * SLOTS) | (listed << 9) | (source << 12) | (1 << FLAG)
        items_v[turn] = jnp.where(mine, item, 0)
        moves[turn].start()
        for n in range(RB):
            rows = pl.ds(n * BS, BS)
            product = lax.dot_general(
                a_ref[turn, rows, SA * BS :], a_ref[turn, rows, : SA * BS], (((0,), (0,)), ((), ())),
                preferred_element_type=F32,
            ).astype(BF16)
            for pair in range(SA // 2):
                left[(turn * RB + n) * (SA // 2) + pair] = product[:, pair * CW : (pair + 1) * CW]
    for copy in tables:
        copy.wait()
    both = p_ref[:, :, pl.ds(PROWS, PAD), :].astype(F32)[:, :, : NX * NC].astype(I32)
    sent_v[...] = jnp.where(my_c == 0, both[:, :, :NX], both[:, :, NX:]).reshape(NZ, NC * NX, CW)
    list_move.start()

    def add_terms(first, turns, block_of, panel_of):
        def pick(at, count):
            for s in range(SA):
                item = items[first + (at >> 3), at & 7, s]
                todo[count] = item
                count = count + (item >> FLAG)
            return count

        count = lax.fori_loop(0, turns * RB, pick, 0)
        for u in range(UNROLL):
            todo[count + u] = 0

        def body(step, unused):
            found = []
            for u in range(UNROLL):
                item = todo[step * UNROLL + u]
                slot = item & (SLOTS * turns - 1)
                block = block_of(item)
                odd = (slot & 1) == 1
                zero = jnp.zeros_like(block)
                right = jnp.concatenate([jnp.where(odd, zero, block), jnp.where(odd, block, zero)], 0)
                term = jnp.dot(left[slot >> 1], right, preferred_element_type=F32)
                found.append((jnp.where((item >> FLAG) == 1, panel_of(item), NX * NZ), term))
            for panel, term in found:
                acc[panel] += term
            return 0

        lax.fori_loop(0, (count + UNROLL - 1) // UNROLL, body, 0)

    def near_block(item):
        entry = (item >> 7) & 127
        listed = jnp.maximum(entry - RB, 0)
        member = jnp.where(entry < RB, my_y, listed >> 3)
        row = jnp.where(entry < RB, entry, need[listed])
        return near_ref[member, pl.ds(pl.multiple_of(row * BS, BS), BS), :]

    def far_block(item):
        panel = (item >> 12) & 15
        group = (my_x - ((item >> 7) & 3)) & (NX - 1)
        row = sent[panel >> 1, (panel & 1) * NX + group, my_z * GP + ((item >> 9) & 7)]
        return p_ref[panel >> 1, panel & 1, pl.ds(pl.multiple_of(row * BS, BS), BS), :]

    near_copy.wait()
    moves[NX].wait()
    add_terms(NX, 1, near_block, lambda item: (my_z >> 1) * NC + my_c)
    for turn in range(NX):
        moves[turn].wait()
    list_move.wait()
    add_terms(0, NX, far_block, lambda item: ((item >> 7) & 3) * NZ + ((item >> 14) & 3) * NC + ((item >> 12) & 1))
    for turn in range(NX):
        group = (my_x - turn) & (NX - 1)
        for at in range(NZ):
            o_ref[group, at // NC, at % NC] = acc[turn * NZ + at].astype(BF16)


def hop(array, axis, size, step):
    return lax.ppermute(array, axis, [(i, (i + step) % size) for i in range(size)])


def shards(a_blocks, p_blocks, a_cols, a_live, group_need, row_send):
    my_z, my_x, my_c, my_y = (lax.axis_index(axis).astype(I32) for axis in ("z", "x", "c", ("yh", "yl")))
    own_p = p_blocks.reshape(PROWS, CW)
    hbm, vmem, smem = (pl.BlockSpec(memory_space=space) for space in (pl.ANY, pltpu.VMEM, pltpu.SMEM))

    by_core = row_send.reshape(NZ, NX, NC, GP).transpose(0, 2, 1, 3).reshape(NZ, NC * NX, GP)
    own, message = pl.pallas_call(
        pack_kernel,
        out_shape=(jax.ShapeDtypeStruct((ROWS, AW), BF16), jax.ShapeDtypeStruct((ROWS, CW), BF16)),
        in_specs=[smem, vmem, vmem, vmem, vmem],
        out_specs=(vmem, vmem),
        name="pack",
    )(a_live, a_blocks.reshape(PROWS, SA * BS), own_p, a_cols, by_core)

    low = hop(own, "x", NX, 1)
    high = hop(own, "x", NX, -1)
    near_p = lax.all_to_all(
        jnp.broadcast_to(own_p[None], (NY, PROWS, CW)), ("yh", "yl"), split_axis=0, concat_axis=0, tiled=True
    )

    around = [(z * NC + c, (z + 1 - 2 * c) % NZ * NC + c) for z in range(NZ) for c in range(NC)]
    beside = hop(message, "c", NC, 1)
    here = jnp.where(my_c == 0, jnp.stack([message, beside]), jnp.stack([beside, message]))
    one = lax.ppermute(here, ("z", "c"), around)
    two = lax.ppermute(one, ("z", "c"), around)
    three = lax.ppermute(two, ("z", "c"), around)
    four = lax.ppermute(three, ("z", "c"), around)
    crossed = hop(jnp.stack([one, two, three]), "c", NC, 1)
    last = lax.ppermute(
        jnp.where(my_c == 0, low, high),
        ("x", "c"),
        [(x * NC + c, (x + 1 - 2 * c) % NX * NC + c) for x in range(NX) for c in range(NC)],
    )

    def terms(odd_z):
        return pl.pallas_call(
            terms_kernel,
            out_shape=jax.ShapeDtypeStruct((NX, NZ // 2, NC, CW, CW), BF16),
            in_specs=[smem, smem, vmem] + [hbm] * 11,
            out_specs=vmem,
            scratch_shapes=[
                pltpu.VMEM((NX, ROWS, AW), BF16),
                pltpu.VMEM((NZ, NC, ROWS, CW), BF16),
                pltpu.VMEM((NY, PROWS, CW), BF16),
                pltpu.VMEM((NX * SLOTS // 2, CW, CW), BF16),
                pltpu.VMEM((NX * NZ + 1, CW, CW), F32),
                pltpu.VMEM((NX + 1, RB, CW), I32),
                pltpu.VMEM((NZ, NC * NX, CW), I32),
                pltpu.SMEM((NX + 1, RB, CW), I32),
                pltpu.SMEM((NZ, NC * NX, CW), I32),
                pltpu.SMEM((NX * SLOTS + UNROLL,), I32),
                pltpu.SemaphoreType.DMA((2 * NX + NZ + 3,)),
            ],
            compiler_params=pltpu.CompilerParams(vmem_limit_bytes=56 * 1024 * 1024),
            cost_estimate=pl.CostEstimate(flops=2 * 10**9, bytes_accessed=12 * 10**6, transcendentals=0),
            name="terms",
        )(
            jnp.stack([my_z, my_x, my_c, my_y, a_live[0], odd_z]), group_need.reshape(-1), a_cols,
            own, low, last, high, here, one, two, three, four, crossed, near_p,
        )

    pairs = [
        (c * NY + y, c * NY + (y + 1 - 2 * ((y + c) & 1)) % NY) for c in range(NC) for y in range(NY)
    ]
    given = lax.ppermute(terms(1 - (my_y & 1)), ("c", "yh", "yl"), pairs)
    kept = terms(my_y & 1)
    partial = (kept.astype(F32) + given.astype(F32)).astype(BF16)

    parts = lax.all_to_all(
        partial.reshape(NX * NY // 2, NC, CW, CW), ("x", "yh"), split_axis=0, concat_axis=0, tiled=True
    ).reshape(NX, NY // 2, NC, CW, CW)
    total = jnp.sum(parts.astype(F32), axis=1).astype(BF16)
    return total.reshape(1, NX * NC, CW, CW)


def solution(mesh):
    split = Mesh(mesh.devices.reshape(NZ, NX, NC, NY // 2, 2), ("z", "x", "c", "yh", "yl"))
    every = ("z", "x", "c", "yh", "yl")
    placed = (
        P(every, None, None),
        P(every, None, None),
        P(every, None),
        P(every),
        P(every, None, None),
        P(every, None, None),
    )
    return jax.shard_map(
        shards, mesh=split, in_specs=placed, out_specs=P(("z", "x", "c"), ("yh", "yl"), None, None), check_vma=False
    )
```

```python
import jax
import jax.numpy as jnp
from jax import lax
from jax.experimental import pallas as pl
from jax.experimental.pallas import tpu as pltpu
from jax.sharding import Mesh, PartitionSpec as P

NZ, NX, NC, NY = 8, 4, 2, 8
RB, BS, CW, SA = 8, 64, 128, 16
GP = 6
NEAR = RB + NY * RB
SLOTS = RB * SA
PAD = 16
PROWS = RB * BS
ROWS = PROWS + PAD
AW = SA * BS + CW
UNROLL = 8
OFF = 255
FLAG = 20
BF16, F32, I32 = jnp.bfloat16, jnp.float32, jnp.int32


def pack_kernel(live, a_ref, p_ref, cols, lists, own_ref, message_ref):
    own_ref[:PROWS, : SA * BS] = a_ref[...]
    own_ref[:PROWS, SA * BS :] = p_ref[...]
    message_ref[:PROWS, :] = p_ref[...]
    message_ref[PROWS:, :] = jnp.zeros((PAD, CW), BF16)
    listed = jnp.concatenate([lists[...], jnp.zeros((PAD - GP, NZ * NX * NC), I32)], 0)
    message_ref[PROWS:, : NZ * NX * NC] = listed.astype(F32).astype(BF16)
    entry = cols[...] - NEAR
    far = (entry >= 0) & (lax.broadcasted_iota(I32, (RB, SA), 0) < live[0])
    entry = jnp.where(far, entry, 0)
    panel = (entry * 10923) >> 16
    codes = jnp.concatenate([jnp.where(far, panel, OFF), entry - panel * GP], 0)
    own_ref[PROWS:, :] = jnp.zeros((PAD, AW), BF16)
    own_ref[PROWS:, :SA] = codes.astype(F32).astype(BF16)


def terms_kernel(place, need, cols, *refs):
    groups_hbm, refs = refs[:NX], refs[NX:]
    here_hbm, one_hbm, two_hbm, three_hbm, four_hbm, crossed_hbm, near_hbm = refs[:7]
    o_ref, a_ref, p_ref, near_ref, left, acc, items_v, sent_v, items, sent, todo, sems = refs[7:]
    my_z, my_x, my_c, my_y, live, odd_z = (place[i] for i in range(6))
    back = 2 * my_c - 1
    copies = [pltpu.make_async_copy(groups_hbm[turn], a_ref.at[turn], sems.at[turn]) for turn in range(NX)]
    sources = [(here_hbm, 0), (one_hbm, back), (two_hbm, 2 * back), (three_hbm, 3 * back), (four_hbm, 4)]
    sources += [(crossed_hbm.at[s], -(s + 1) * back) for s in range(3)]
    tables = [
        pltpu.make_async_copy(source, p_ref.at[(my_z + step) & (NZ - 1)], sems.at[NX + at])
        for at, (source, step) in enumerate(sources)
    ]
    near_copy = pltpu.make_async_copy(near_hbm, near_ref, sems.at[NX + NZ])
    for copy in copies[:1] + tables + [near_copy] + copies[1:]:
        copy.start()
    slots = lax.broadcasted_iota(I32, (RB, CW), 0) * SA + lax.broadcasted_iota(I32, (RB, CW), 1)
    moves = [
        pltpu.make_async_copy(items_v.at[turn], items.at[turn], sems.at[NX + NZ + 1 + turn]) for turn in range(NX + 1)
    ]
    list_move = pltpu.make_async_copy(sent_v, sent, sems.at[2 * NX + NZ + 2])

    entry = cols[...]
    close = (entry < NEAR) & (lax.broadcasted_iota(I32, (RB, SA), 0) < live) & ((my_z & 1) == odd_z)
    items_v[NX, :, :SA] = jnp.where(close, slots[:, :SA] | (entry << 7) | (1 << FLAG), 0)
    moves[NX].start()
    acc[...] = jnp.zeros_like(acc)

    for turn in range(NX):
        copies[turn].wait()
        code = a_ref[turn, pl.ds(PROWS, PAD), :CW].astype(F32).astype(I32)
        panel, listed = code[:RB], code[RB:]
        mine = (panel < OFF) & (((panel >> 1) & (NX - 1)) == my_x) & (((panel >> 3) & 1) == odd_z)
        source = (panel >> 3) * NC + (panel & 1)
        item = (slots + turn * SLOTS) | (listed << 9) | (source << 12) | (1 << FLAG)
        items_v[turn] = jnp.where(mine, item, 0)
        moves[turn].start()
        for n in range(RB):
            rows = pl.ds(n * BS, BS)
            product = lax.dot_general(
                a_ref[turn, rows, SA * BS :], a_ref[turn, rows, : SA * BS], (((0,), (0,)), ((), ())),
                preferred_element_type=F32,
            ).astype(BF16)
            for pair in range(SA // 2):
                left[(turn * RB + n) * (SA // 2) + pair] = product[:, pair * CW : (pair + 1) * CW]
    for copy in tables:
        copy.wait()
    both = p_ref[:, :, pl.ds(PROWS, PAD), :].astype(F32)[:, :, :RB].astype(I32)
    sent_v[...] = both[:, 0] | (both[:, 1] << 3)
    list_move.start()

    def select(first, turns, start):
        def pick(at, count):
            for s in range(SA):
                item = items[first + (at >> 3), at & 7, s]
                todo[start + count] = item
                count = count + (item >> FLAG)
            return count

        count = lax.fori_loop(0, turns * RB, pick, 0)
        for u in range(UNROLL):
            todo[start + count + u] = 0
        return count

    def add_terms(start, count, turns, block_of, panel_of):
        def body(step, unused):
            found = []
            for u in range(UNROLL):
                item = todo[start + step * UNROLL + u]
                slot = item & (SLOTS * turns - 1)
                block = block_of(item)
                odd = (slot & 1) == 1
                zero = jnp.zeros_like(block)
                right = jnp.concatenate([jnp.where(odd, zero, block), jnp.where(odd, block, zero)], 0)
                term = jnp.dot(left[slot >> 1], right, preferred_element_type=F32)
                found.append((jnp.where((item >> FLAG) == 1, panel_of(item), NX * NZ), term))
            for panel, term in found:
                acc[panel] += term
            return 0

        lax.fori_loop(0, (count + UNROLL - 1) // UNROLL, body, 0)

    def near_block(item):
        entry = (item >> 7) & 127
        listed = jnp.maximum(entry - RB, 0)
        member = jnp.where(entry < RB, my_y, listed >> 3)
        row = jnp.where(entry < RB, entry, need[listed])
        return near_ref[member, pl.ds(pl.multiple_of(row * BS, BS), BS), :]

    def far_block(item):
        panel = (item >> 12) & 15
        group = (my_x - ((item >> 7) & 3)) & (NX - 1)
        row = (sent[panel >> 1, (item >> 9) & 7, (my_z * NX + group) * NC + my_c] >> ((panel & 1) * 3)) & 7
        return p_ref[panel >> 1, panel & 1, pl.ds(pl.multiple_of(row * BS, BS), BS), :]

    for move in moves:
        move.wait()
    near_start = NX * SLOTS + UNROLL
    near_count = select(NX, 1, near_start)
    far_count = select(0, NX, 0)
    near_copy.wait()
    add_terms(near_start, near_count, 1, near_block, lambda item: (my_z >> 1) * NC + my_c)
    list_move.wait()
    add_terms(
        0, far_count, NX, far_block,
        lambda item: ((item >> 7) & 3) * NZ + ((item >> 14) & 3) * NC + ((item >> 12) & 1),
    )
    for turn in range(NX):
        group = (my_x - turn) & (NX - 1)
        for at in range(NZ):
            o_ref[group, at // NC, at % NC] = acc[turn * NZ + at].astype(BF16)


def hop(array, axis, size, step):
    return lax.ppermute(array, axis, [(i, (i + step) % size) for i in range(size)])


def shards(a_blocks, p_blocks, a_cols, a_live, group_need, row_send):
    my_z, my_x, my_c, my_y = (lax.axis_index(axis).astype(I32) for axis in ("z", "x", "c", ("yh", "yl")))
    own_p = p_blocks.reshape(PROWS, CW)
    hbm, vmem, smem = (pl.BlockSpec(memory_space=space) for space in (pl.ANY, pltpu.VMEM, pltpu.SMEM))

    own, message = pl.pallas_call(
        pack_kernel,
        out_shape=(jax.ShapeDtypeStruct((ROWS, AW), BF16), jax.ShapeDtypeStruct((ROWS, CW), BF16)),
        in_specs=[smem, vmem, vmem, vmem, vmem],
        out_specs=(vmem, vmem),
        name="pack",
    )(a_live, a_blocks.reshape(PROWS, SA * BS), own_p, a_cols, row_send[0].T)

    low = hop(own, "x", NX, 1)
    high = hop(own, "x", NX, -1)
    near_p = lax.all_to_all(
        jnp.broadcast_to(own_p[None], (NY, PROWS, CW)), ("yh", "yl"), split_axis=0, concat_axis=0, tiled=True
    )

    around = [(z * NC + c, (z + 1 - 2 * c) % NZ * NC + c) for z in range(NZ) for c in range(NC)]
    beside = hop(message, "c", NC, 1)
    here = jnp.where(my_c == 0, jnp.stack([message, beside]), jnp.stack([beside, message]))
    one = lax.ppermute(here, ("z", "c"), around)
    two = lax.ppermute(one, ("z", "c"), around)
    three = lax.ppermute(two, ("z", "c"), around)
    four = lax.ppermute(three, ("z", "c"), around)
    crossed = hop(jnp.stack([one, two, three]), "c", NC, 1)
    last = lax.ppermute(
        jnp.where(my_c == 0, low, high),
        ("x", "c"),
        [(x * NC + c, (x + 1 - 2 * c) % NX * NC + c) for x in range(NX) for c in range(NC)],
    )

    def terms(odd_z):
        return pl.pallas_call(
            terms_kernel,
            out_shape=jax.ShapeDtypeStruct((NX, NZ // 2, NC, CW, CW), BF16),
            in_specs=[smem, smem, vmem] + [hbm] * 11,
            out_specs=vmem,
            scratch_shapes=[
                pltpu.VMEM((NX, ROWS, AW), BF16),
                pltpu.VMEM((NZ, NC, ROWS, CW), BF16),
                pltpu.VMEM((NY, PROWS, CW), BF16),
                pltpu.VMEM((NX * SLOTS // 2, CW, CW), BF16),
                pltpu.VMEM((NX * NZ + 1, CW, CW), F32),
                pltpu.VMEM((NX + 1, RB, CW), I32),
                pltpu.VMEM((NZ, NC * NX, CW), I32),
                pltpu.SMEM((NX + 1, RB, CW), I32),
                pltpu.SMEM((NZ, NC * NX, CW), I32),
                pltpu.SMEM(((NX + 1) * SLOTS + 2 * UNROLL,), I32),
                pltpu.SemaphoreType.DMA((2 * NX + NZ + 3,)),
            ],
            compiler_params=pltpu.CompilerParams(vmem_limit_bytes=56 * 1024 * 1024),
            cost_estimate=pl.CostEstimate(flops=2 * 10**9, bytes_accessed=12 * 10**6, transcendentals=0),
            name="terms",
        )(
            jnp.stack([my_z, my_x, my_c, my_y, a_live[0], odd_z]), group_need.reshape(-1), a_cols,
            own, low, last, high, here, one, two, three, four, crossed, near_p,
        )

    pairs = [
        (c * NY + y, c * NY + (y + 1 - 2 * ((y + c) & 1)) % NY) for c in range(NC) for y in range(NY)
    ]
    given = lax.ppermute(terms(1 - (my_y & 1)), ("c", "yh", "yl"), pairs)
    kept = terms(my_y & 1)
    partial = (kept.astype(F32) + given.astype(F32)).astype(BF16)

    parts = lax.all_to_all(
        partial.reshape(NX * NY // 2, NC, CW, CW), ("x", "yh"), split_axis=0, concat_axis=0, tiled=True
    ).reshape(NX, NY // 2, NC, CW, CW)
    total = jnp.sum(parts.astype(F32), axis=1).astype(BF16)
    return total.reshape(1, NX * NC, CW, CW)


def solution(mesh):
    split = Mesh(mesh.devices.reshape(NZ, NX, NC, NY // 2, 2), ("z", "x", "c", "yh", "yl"))
    every = ("z", "x", "c", "yh", "yl")
    placed = (
        P(every, None, None),
        P(every, None, None),
        P(every, None),
        P(every),
        P(every, None, None),
        P(every, None, None),
    )
    return jax.shard_map(
        shards, mesh=split, in_specs=placed, out_specs=P(("z", "x", "c"), ("yh", "yl"), None, None), check_vma=False
    )
```

```python
import jax
import jax.numpy as jnp
from jax import lax
from jax.experimental import pallas as pl
from jax.experimental.pallas import tpu as pltpu
from jax.sharding import Mesh, PartitionSpec as P

NZ, NX, NC, NY = 8, 4, 2, 8
RB, BS, CW, SA = 8, 64, 128, 16
GP = 6
NEAR = RB + NY * RB
SLOTS = RB * SA
PAD = 16
PROWS = RB * BS
ROWS = PROWS + PAD
AW = SA * BS + CW
UNROLL = 8
OFF = 255
FLAG = 20
BF16, F32, I32 = jnp.bfloat16, jnp.float32, jnp.int32


def pack_kernel(live, a_ref, p_ref, cols, lists, own_ref, message_ref):
    own_ref[:PROWS, : SA * BS] = a_ref[...]
    own_ref[:PROWS, SA * BS :] = p_ref[...]
    message_ref[:PROWS, :] = p_ref[...]
    message_ref[PROWS:, :] = jnp.zeros((PAD, CW), BF16)
    listed = jnp.concatenate([lists[...], jnp.zeros((PAD - GP, NZ * NX * NC), I32)], 0)
    message_ref[PROWS:, : NZ * NX * NC] = listed.astype(F32).astype(BF16)
    entry = cols[...] - NEAR
    far = (entry >= 0) & (lax.broadcasted_iota(I32, (RB, SA), 0) < live[0])
    entry = jnp.where(far, entry, 0)
    panel = (entry * 10923) >> 16
    codes = jnp.concatenate([jnp.where(far, panel, OFF), entry - panel * GP], 0)
    own_ref[PROWS:, :] = jnp.zeros((PAD, AW), BF16)
    own_ref[PROWS:, :SA] = codes.astype(F32).astype(BF16)


def terms_kernel(place, need, cols, *refs):
    groups_hbm, refs = refs[:NX], refs[NX:]
    here_hbm, one_hbm, two_hbm, three_hbm, four_hbm, crossed_hbm, near_hbm = refs[:7]
    o_ref, a_ref, p_ref, near_ref, left, acc, items_v, sent_v, items, sent, todo, sems = refs[7:]
    my_z, my_x, my_c, my_y, live, odd_z = (place[i] for i in range(6))
    back = 2 * my_c - 1
    copies = [pltpu.make_async_copy(groups_hbm[turn], a_ref.at[turn], sems.at[turn]) for turn in range(NX)]
    sources = [(here_hbm, 0), (one_hbm, back), (two_hbm, 2 * back), (three_hbm, 3 * back), (four_hbm, 4)]
    spots = [(source, p_ref.at[(my_z + step) & (NZ - 1)]) for source, step in sources]
    spots += [
        (crossed_hbm.at[s, 1 - c], p_ref.at[(my_z - (s + 1) * back) & (NZ - 1), c]) for s in range(3) for c in range(NC)
    ]
    tables = [pltpu.make_async_copy(*spot, sems.at[NX + at]) for at, spot in enumerate(spots)]
    after = NX + len(tables)
    near_copy = pltpu.make_async_copy(near_hbm, near_ref, sems.at[after])
    for copy in copies[:1] + tables + [near_copy] + copies[1:]:
        copy.start()
    slots = lax.broadcasted_iota(I32, (RB, CW), 0) * SA + lax.broadcasted_iota(I32, (RB, CW), 1)
    moves = [
        pltpu.make_async_copy(items_v.at[turn], items.at[turn], sems.at[after + 1 + turn]) for turn in range(NX + 1)
    ]
    list_move = pltpu.make_async_copy(sent_v, sent, sems.at[after + NX + 2])

    entry = cols[...]
    close = (entry < NEAR) & (lax.broadcasted_iota(I32, (RB, SA), 0) < live) & ((my_z & 1) == odd_z)
    items_v[NX, :, :SA] = jnp.where(close, slots[:, :SA] | (entry << 7) | (1 << FLAG), 0)
    moves[NX].start()
    acc[...] = jnp.zeros_like(acc)

    for turn in range(NX):
        copies[turn].wait()
        code = a_ref[turn, pl.ds(PROWS, PAD), :CW].astype(F32).astype(I32)
        panel, listed = code[:RB], code[RB:]
        mine = (panel < OFF) & (((panel >> 1) & (NX - 1)) == my_x) & (((panel >> 3) & 1) == odd_z)
        source = (panel >> 3) * NC + (panel & 1)
        item = (slots + turn * SLOTS) | (listed << 9) | (source << 12) | (1 << FLAG)
        items_v[turn] = jnp.where(mine, item, 0)
        moves[turn].start()
        for n in range(RB):
            rows = pl.ds(n * BS, BS)
            product = lax.dot_general(
                a_ref[turn, rows, SA * BS :], a_ref[turn, rows, : SA * BS], (((0,), (0,)), ((), ())),
                preferred_element_type=F32,
            ).astype(BF16)
            for pair in range(SA // 2):
                left[(turn * RB + n) * (SA // 2) + pair] = product[:, pair * CW : (pair + 1) * CW]
    for copy in tables:
        copy.wait()
    both = p_ref[:, :, pl.ds(PROWS, PAD), :].astype(F32)[:, :, :RB].astype(I32)
    sent_v[...] = both[:, 0] | (both[:, 1] << 3)
    list_move.start()

    def select(first, turns, start):
        def pick(at, count):
            for s in range(SA):
                item = items[first + (at >> 3), at & 7, s]
                todo[start + count] = item
                count = count + (item >> FLAG)
            return count

        count = lax.fori_loop(0, turns * RB, pick, 0)
        for u in range(UNROLL):
            todo[start + count + u] = 0
        return count

    def add_terms(start, count, turns, block_of, panel_of):
        def body(step, unused):
            found = []
            for u in range(UNROLL):
                item = todo[start + step * UNROLL + u]
                slot = item & (SLOTS * turns - 1)
                block = block_of(item)
                odd = (slot & 1) == 1
                zero = jnp.zeros_like(block)
                right = jnp.concatenate([jnp.where(odd, zero, block), jnp.where(odd, block, zero)], 0)
                term = jnp.dot(left[slot >> 1], right, preferred_element_type=F32)
                found.append((jnp.where((item >> FLAG) == 1, panel_of(item), NX * NZ), term))
            for panel, term in found:
                acc[panel] += term
            return 0

        lax.fori_loop(0, (count + UNROLL - 1) // UNROLL, body, 0)

    def near_block(item):
        entry = (item >> 7) & 127
        listed = jnp.maximum(entry - RB, 0)
        member = jnp.where(entry < RB, my_y, listed >> 3)
        row = jnp.where(entry < RB, entry, need[listed])
        return near_ref[member, pl.ds(pl.multiple_of(row * BS, BS), BS), :]

    def far_block(item):
        panel = (item >> 12) & 15
        group = (my_x - ((item >> 7) & 3)) & (NX - 1)
        other = (panel & 1) ^ my_c
        row = (sent[panel >> 1, (item >> 9) & 7, (my_z * NX + group) * NC + my_c] >> (other * 3)) & 7
        return p_ref[panel >> 1, other, pl.ds(pl.multiple_of(row * BS, BS), BS), :]

    for move in moves:
        move.wait()
    near_start = NX * SLOTS + UNROLL
    near_count = select(NX, 1, near_start)
    far_count = select(0, NX, 0)
    near_copy.wait()
    add_terms(near_start, near_count, 1, near_block, lambda item: (my_z >> 1) * NC + my_c)
    list_move.wait()
    add_terms(
        0, far_count, NX, far_block,
        lambda item: ((item >> 7) & 3) * NZ + ((item >> 14) & 3) * NC + ((item >> 12) & 1),
    )
    for turn in range(NX):
        group = (my_x - turn) & (NX - 1)
        for at in range(NZ):
            o_ref[group, at // NC, at % NC] = acc[turn * NZ + at].astype(BF16)


def hop(array, axis, size, step):
    return lax.ppermute(array, axis, [(i, (i + step) % size) for i in range(size)])


def shards(a_blocks, p_blocks, a_cols, a_live, group_need, row_send):
    my_z, my_x, my_c, my_y = (lax.axis_index(axis).astype(I32) for axis in ("z", "x", "c", ("yh", "yl")))
    own_p = p_blocks.reshape(PROWS, CW)
    hbm, vmem, smem = (pl.BlockSpec(memory_space=space) for space in (pl.ANY, pltpu.VMEM, pltpu.SMEM))

    own, message = pl.pallas_call(
        pack_kernel,
        out_shape=(jax.ShapeDtypeStruct((ROWS, AW), BF16), jax.ShapeDtypeStruct((ROWS, CW), BF16)),
        in_specs=[smem, vmem, vmem, vmem, vmem],
        out_specs=(vmem, vmem),
        name="pack",
    )(a_live, a_blocks.reshape(PROWS, SA * BS), own_p, a_cols, row_send[0].T)

    low = hop(own, "x", NX, 1)
    high = hop(own, "x", NX, -1)
    near_p = lax.all_to_all(
        jnp.broadcast_to(own_p[None], (NY, PROWS, CW)), ("yh", "yl"), split_axis=0, concat_axis=0, tiled=True
    )

    around = [(z * NC + c, (z + 1 - 2 * c) % NZ * NC + c) for z in range(NZ) for c in range(NC)]
    beside = hop(message, "c", NC, 1)
    here = jnp.stack([message, beside])
    one = lax.ppermute(here, ("z", "c"), around)
    two = lax.ppermute(one, ("z", "c"), around)
    three = lax.ppermute(two, ("z", "c"), around)
    four = lax.ppermute(three, ("z", "c"), around)
    crossed = hop(jnp.stack([one, two, three]), "c", NC, 1)
    last = lax.ppermute(
        jnp.where(my_c == 0, low, high),
        ("x", "c"),
        [(x * NC + c, (x + 1 - 2 * c) % NX * NC + c) for x in range(NX) for c in range(NC)],
    )

    def terms(odd_z):
        return pl.pallas_call(
            terms_kernel,
            out_shape=jax.ShapeDtypeStruct((NX, NZ // 2, NC, CW, CW), BF16),
            in_specs=[smem, smem, vmem] + [hbm] * 11,
            out_specs=vmem,
            scratch_shapes=[
                pltpu.VMEM((NX, ROWS, AW), BF16),
                pltpu.VMEM((NZ, NC, ROWS, CW), BF16),
                pltpu.VMEM((NY, PROWS, CW), BF16),
                pltpu.VMEM((NX * SLOTS // 2, CW, CW), BF16),
                pltpu.VMEM((NX * NZ + 1, CW, CW), F32),
                pltpu.VMEM((NX + 1, RB, CW), I32),
                pltpu.VMEM((NZ, NC * NX, CW), I32),
                pltpu.SMEM((NX + 1, RB, CW), I32),
                pltpu.SMEM((NZ, NC * NX, CW), I32),
                pltpu.SMEM(((NX + 1) * SLOTS + 2 * UNROLL,), I32),
                pltpu.SemaphoreType.DMA((2 * NX + NZ + 6,)),
            ],
            compiler_params=pltpu.CompilerParams(vmem_limit_bytes=56 * 1024 * 1024),
            cost_estimate=pl.CostEstimate(flops=2 * 10**9, bytes_accessed=12 * 10**6, transcendentals=0),
            name="terms",
        )(
            jnp.stack([my_z, my_x, my_c, my_y, a_live[0], odd_z]), group_need.reshape(-1), a_cols,
            own, low, last, high, here, one, two, three, four, crossed, near_p,
        )

    pairs = [
        (c * NY + y, c * NY + (y + 1 - 2 * ((y + c) & 1)) % NY) for c in range(NC) for y in range(NY)
    ]
    given = lax.ppermute(terms(1 - (my_y & 1)), ("c", "yh", "yl"), pairs)
    kept = terms(my_y & 1)
    partial = (kept.astype(F32) + given.astype(F32)).astype(BF16)

    parts = lax.all_to_all(
        partial.reshape(NX * NY // 2, NC, CW, CW), ("x", "yh"), split_axis=0, concat_axis=0, tiled=True
    ).reshape(NX, NY // 2, NC, CW, CW)
    total = jnp.sum(parts.astype(F32), axis=1).astype(BF16)
    return total.reshape(1, NX * NC, CW, CW)


def solution(mesh):
    split = Mesh(mesh.devices.reshape(NZ, NX, NC, NY // 2, 2), ("z", "x", "c", "yh", "yl"))
    every = ("z", "x", "c", "yh", "yl")
    placed = (
        P(every, None, None),
        P(every, None, None),
        P(every, None),
        P(every),
        P(every, None, None),
        P(every, None, None),
    )
    return jax.shard_map(
        shards, mesh=split, in_specs=placed, out_specs=P(("z", "x", "c"), ("yh", "yl"), None, None), check_vma=False
    )
```

```python
import jax
import jax.numpy as jnp
from jax import lax
from jax.experimental import pallas as pl
from jax.experimental.pallas import tpu as pltpu
from jax.sharding import Mesh, PartitionSpec as P

NZ, NX, NC, NY = 8, 4, 2, 8
RB, BS, CW, SA = 8, 64, 128, 16
GP = 6
NEAR = RB + NY * RB
SLOTS = RB * SA
PAD = 16
PROWS = RB * BS
ROWS = PROWS + PAD
AW = SA * BS + CW
UNROLL = 8
OFF = 255
FLAG = 20
BF16, F32, I32 = jnp.bfloat16, jnp.float32, jnp.int32


def pack_kernel(live, a_ref, p_ref, cols, lists, own_ref, message_ref):
    own_ref[:PROWS, : SA * BS] = a_ref[...]
    own_ref[:PROWS, SA * BS :] = p_ref[...]
    message_ref[:PROWS, :] = p_ref[...]
    message_ref[PROWS:, :] = jnp.zeros((PAD, CW), BF16)
    listed = jnp.concatenate([lists[...], jnp.zeros((PAD - GP, NZ * NX * NC), I32)], 0)
    message_ref[PROWS:, : NZ * NX * NC] = listed.astype(F32).astype(BF16)
    entry = cols[...] - NEAR
    far = (entry >= 0) & (lax.broadcasted_iota(I32, (RB, SA), 0) < live[0])
    entry = jnp.where(far, entry, 0)
    panel = (entry * 10923) >> 16
    codes = jnp.concatenate([jnp.where(far, panel, OFF), entry - panel * GP], 0)
    own_ref[PROWS:, :] = jnp.zeros((PAD, AW), BF16)
    own_ref[PROWS:, :SA] = codes.astype(F32).astype(BF16)


def terms_kernel(place, need, cols, *refs):
    groups_hbm, refs = refs[:NX], refs[NX:]
    here_hbm, one_hbm, two_hbm, three_hbm, four_hbm, crossed_hbm, near_hbm = refs[:7]
    o_ref, a_ref, p_ref, near_ref, left, acc, items_v, sent_v, items, sent, todo, sems = refs[7:]
    my_z, my_x, my_c, my_y, live, odd_z = (place[i] for i in range(6))
    back = 2 * my_c - 1
    copies = [pltpu.make_async_copy(groups_hbm[turn], a_ref.at[turn], sems.at[turn]) for turn in range(NX)]
    sources = [(here_hbm, 0), (one_hbm, back), (two_hbm, 2 * back), (three_hbm, 3 * back), (four_hbm, 4)]
    spots = [(source, p_ref.at[(my_z + step) & (NZ - 1)]) for source, step in sources]
    spots += [
        (crossed_hbm.at[s, 1 - c], p_ref.at[(my_z - (s + 1) * back) & (NZ - 1), c]) for s in range(3) for c in range(NC)
    ]
    tables = [pltpu.make_async_copy(*spot, sems.at[NX + at]) for at, spot in enumerate(spots)]
    after = NX + len(tables)
    near_copy = pltpu.make_async_copy(near_hbm, near_ref, sems.at[after])
    for copy in copies[:1] + [near_copy] + copies[1:] + tables:
        copy.start()
    slots = lax.broadcasted_iota(I32, (RB, CW), 0) * SA + lax.broadcasted_iota(I32, (RB, CW), 1)
    moves = [
        pltpu.make_async_copy(items_v.at[turn], items.at[turn], sems.at[after + 1 + turn]) for turn in range(NX + 1)
    ]
    list_move = pltpu.make_async_copy(sent_v, sent, sems.at[after + NX + 2])

    entry = cols[...]
    close = (entry < NEAR) & (lax.broadcasted_iota(I32, (RB, SA), 0) < live) & ((my_z & 1) == odd_z)
    items_v[NX, :, :SA] = jnp.where(close, slots[:, :SA] | (entry << 7) | (1 << FLAG), 0)
    moves[NX].start()
    acc[...] = jnp.zeros_like(acc)
    near_start = NX * SLOTS + UNROLL

    def select(first, turns, start):
        def pick(at, count):
            for s in range(SA):
                item = items[first + (at >> 3), at & 7, s]
                todo[start + count] = item
                count = count + (item >> FLAG)
            return count

        count = lax.fori_loop(0, turns * RB, pick, 0)
        for u in range(UNROLL):
            todo[start + count + u] = 0
        return count

    def add_terms(start, count, turns, block_of, panel_of):
        def body(step, unused):
            found = []
            for u in range(UNROLL):
                item = todo[start + step * UNROLL + u]
                slot = item & (SLOTS * turns - 1)
                block = block_of(item)
                odd = (slot & 1) == 1
                zero = jnp.zeros_like(block)
                right = jnp.concatenate([jnp.where(odd, zero, block), jnp.where(odd, block, zero)], 0)
                term = jnp.dot(left[slot >> 1], right, preferred_element_type=F32)
                found.append((jnp.where((item >> FLAG) == 1, panel_of(item), NX * NZ), term))
            for panel, term in found:
                acc[panel] += term
            return 0

        lax.fori_loop(0, (count + UNROLL - 1) // UNROLL, body, 0)

    def near_block(item):
        entry = (item >> 7) & 127
        listed = jnp.maximum(entry - RB, 0)
        member = jnp.where(entry < RB, my_y, listed >> 3)
        row = jnp.where(entry < RB, entry, need[listed])
        return near_ref[member, pl.ds(pl.multiple_of(row * BS, BS), BS), :]

    def far_block(item):
        panel = (item >> 12) & 15
        group = (my_x - ((item >> 7) & 3)) & (NX - 1)
        other = (panel & 1) ^ my_c
        row = (sent[panel >> 1, (item >> 9) & 7, (my_z * NX + group) * NC + my_c] >> (other * 3)) & 7
        return p_ref[panel >> 1, other, pl.ds(pl.multiple_of(row * BS, BS), BS), :]

    for turn in range(NX):
        copies[turn].wait()
        code = a_ref[turn, pl.ds(PROWS, PAD), :CW].astype(F32).astype(I32)
        panel, listed = code[:RB], code[RB:]
        mine = (panel < OFF) & (((panel >> 1) & (NX - 1)) == my_x) & (((panel >> 3) & 1) == odd_z)
        source = (panel >> 3) * NC + (panel & 1)
        item = (slots + turn * SLOTS) | (listed << 9) | (source << 12) | (1 << FLAG)
        items_v[turn] = jnp.where(mine, item, 0)
        moves[turn].start()
        for n in range(RB):
            rows = pl.ds(n * BS, BS)
            product = lax.dot_general(
                a_ref[turn, rows, SA * BS :], a_ref[turn, rows, : SA * BS], (((0,), (0,)), ((), ())),
                preferred_element_type=F32,
            ).astype(BF16)
            for pair in range(SA // 2):
                left[(turn * RB + n) * (SA // 2) + pair] = product[:, pair * CW : (pair + 1) * CW]
        if turn == 0:
            moves[NX].wait()
            near_count = select(NX, 1, near_start)
            near_copy.wait()
            add_terms(near_start, near_count, 1, near_block, lambda item: (my_z >> 1) * NC + my_c)
    for copy in tables:
        copy.wait()
    both = p_ref[:, :, pl.ds(PROWS, PAD), :].astype(F32)[:, :, :RB].astype(I32)
    sent_v[...] = both[:, 0] | (both[:, 1] << 3)
    list_move.start()
    for move in moves[:NX]:
        move.wait()
    far_count = select(0, NX, 0)
    list_move.wait()
    add_terms(
        0, far_count, NX, far_block,
        lambda item: ((item >> 7) & 3) * NZ + ((item >> 14) & 3) * NC + ((item >> 12) & 1),
    )
    for turn in range(NX):
        group = (my_x - turn) & (NX - 1)
        for at in range(NZ):
            o_ref[group, at // NC, at % NC] = acc[turn * NZ + at].astype(BF16)


def hop(array, axis, size, step):
    return lax.ppermute(array, axis, [(i, (i + step) % size) for i in range(size)])


def shards(a_blocks, p_blocks, a_cols, a_live, group_need, row_send):
    my_z, my_x, my_c, my_y = (lax.axis_index(axis).astype(I32) for axis in ("z", "x", "c", ("yh", "yl")))
    own_p = p_blocks.reshape(PROWS, CW)
    hbm, vmem, smem = (pl.BlockSpec(memory_space=space) for space in (pl.ANY, pltpu.VMEM, pltpu.SMEM))

    own, message = pl.pallas_call(
        pack_kernel,
        out_shape=(jax.ShapeDtypeStruct((ROWS, AW), BF16), jax.ShapeDtypeStruct((ROWS, CW), BF16)),
        in_specs=[smem, vmem, vmem, vmem, vmem],
        out_specs=(vmem, vmem),
        name="pack",
    )(a_live, a_blocks.reshape(PROWS, SA * BS), own_p, a_cols, row_send[0].T)

    low = hop(own, "x", NX, 1)
    high = hop(own, "x", NX, -1)
    near_p = lax.all_to_all(
        jnp.broadcast_to(own_p[None], (NY, PROWS, CW)), ("yh", "yl"), split_axis=0, concat_axis=0, tiled=True
    )

    around = [(z * NC + c, (z + 1 - 2 * c) % NZ * NC + c) for z in range(NZ) for c in range(NC)]
    beside = hop(message, "c", NC, 1)
    here = jnp.stack([message, beside])
    one = lax.ppermute(here, ("z", "c"), around)
    two = lax.ppermute(one, ("z", "c"), around)
    three = lax.ppermute(two, ("z", "c"), around)
    four = lax.ppermute(three, ("z", "c"), around)
    crossed = hop(jnp.stack([one, two, three]), "c", NC, 1)
    last = lax.ppermute(
        jnp.where(my_c == 0, low, high),
        ("x", "c"),
        [(x * NC + c, (x + 1 - 2 * c) % NX * NC + c) for x in range(NX) for c in range(NC)],
    )

    def terms(odd_z):
        return pl.pallas_call(
            terms_kernel,
            out_shape=jax.ShapeDtypeStruct((NX, NZ // 2, NC, CW, CW), BF16),
            in_specs=[smem, smem, vmem] + [hbm] * 11,
            out_specs=vmem,
            scratch_shapes=[
                pltpu.VMEM((NX, ROWS, AW), BF16),
                pltpu.VMEM((NZ, NC, ROWS, CW), BF16),
                pltpu.VMEM((NY, PROWS, CW), BF16),
                pltpu.VMEM((NX * SLOTS // 2, CW, CW), BF16),
                pltpu.VMEM((NX * NZ + 1, CW, CW), F32),
                pltpu.VMEM((NX + 1, RB, CW), I32),
                pltpu.VMEM((NZ, NC * NX, CW), I32),
                pltpu.SMEM((NX + 1, RB, CW), I32),
                pltpu.SMEM((NZ, NC * NX, CW), I32),
                pltpu.SMEM(((NX + 1) * SLOTS + 2 * UNROLL,), I32),
                pltpu.SemaphoreType.DMA((2 * NX + NZ + 6,)),
            ],
            compiler_params=pltpu.CompilerParams(vmem_limit_bytes=56 * 1024 * 1024),
            cost_estimate=pl.CostEstimate(flops=2 * 10**9, bytes_accessed=12 * 10**6, transcendentals=0),
            name="terms",
        )(
            jnp.stack([my_z, my_x, my_c, my_y, a_live[0], odd_z]), group_need.reshape(-1), a_cols,
            own, low, last, high, here, one, two, three, four, crossed, near_p,
        )

    pairs = [
        (c * NY + y, c * NY + (y + 1 - 2 * ((y + c) & 1)) % NY) for c in range(NC) for y in range(NY)
    ]
    given = lax.ppermute(terms(1 - (my_y & 1)), ("c", "yh", "yl"), pairs)
    kept = terms(my_y & 1)
    partial = (kept.astype(F32) + given.astype(F32)).astype(BF16)

    parts = lax.all_to_all(
        partial.reshape(NX * NY // 2, NC, CW, CW), ("x", "yh"), split_axis=0, concat_axis=0, tiled=True
    ).reshape(NX, NY // 2, NC, CW, CW)
    total = jnp.sum(parts.astype(F32), axis=1).astype(BF16)
    return total.reshape(1, NX * NC, CW, CW)


def solution(mesh):
    split = Mesh(mesh.devices.reshape(NZ, NX, NC, NY // 2, 2), ("z", "x", "c", "yh", "yl"))
    every = ("z", "x", "c", "yh", "yl")
    placed = (
        P(every, None, None),
        P(every, None, None),
        P(every, None),
        P(every),
        P(every, None, None),
        P(every, None, None),
    )
    return jax.shard_map(
        shards, mesh=split, in_specs=placed, out_specs=P(("z", "x", "c"), ("yh", "yl"), None, None), check_vma=False
    )
```
